32 devices in a mesh: dp: 8 (over y, x, core), tensor: 4 (over z).
Axes of the slice: x: 2, y: 2, z: 4, core: 2. Of those that a mesh axis runs over, the one named last changes fastest.
Arguments:
- activations: bfloat16 [2, 128, 8192], P(None, 'dp', 'tensor'), may hold values from -6 to 6
- gate_weight: bfloat16 [8192, 28672], P('tensor', 'dp'), may hold values from -0.0625 to 0.0625
- up_weight: bfloat16 [8192, 28672], P('tensor', 'dp'), may hold values from -0.0625 to 0.0625
- down_weight: bfloat16 [28672, 8192], P('dp', 'tensor'), may hold values from -0.03125 to 0.03125
- shrink_weight: bfloat16 [8192, 1024], P('tensor', 'dp'), may hold values from -0.0625 to 0.0625
- expand_weight: bfloat16 [2, 32, 16, 28672], P(None, 'tensor', None, 'dp'), may hold values from -1.5 to 1.5
- adapter_scale: float32 [32], P('dp'), may hold values from 0.5 to 2
- adapter_ids: int32 [128], replicated, may hold values from 0 to 31, as said below
Outputs:
- mixed: bfloat16 [2, 128, 8192], P(None, 'dp', 'tensor')
The draws below stay inside these ranges and needn't reach their ends.
Inputs may be any that keep to these rules, and one draw needn't show every extreme that they name: `adapter_ids`: at most 64 rows name adapters of one adapter block of 8 consecutive adapters, and in every draw some block is named by exactly 64 rows.
All inputs are finite; a program needn't handle non-finite values.
Results may differ from the reference program's by a relative error of at most 0.03.
Values may be sent and summed in bfloat16 or wider, within the bound.
No kernel may reach another device: no remote copies, remote signals or barrier semaphores. Data moves between devices by JAX's collectives and lax.ppermute only.
A program may use at most 128 MiB of HBM per device.

```python
import math
import jax
import jax.numpy as jnp
from jax import lax

D = 8192
FF = 28672
R = 16
STEPS = 2
ROWS = 128
ADAPTERS = 32
ADP_T = 8
CAP_T = 64
N_TENSOR = 4


def draw_adapter_ids(key, part):
    key_hot, key_order, key_slots, key_local = jax.random.split(key, 4)
    blocks = ADAPTERS // ADP_T
    hot_block = jax.random.randint(key_hot, (), 0, blocks)
    position = jax.random.permutation(key_order, ROWS)
    slot_order = jax.random.permutation(key_slots, (blocks - 1) * CAP_T)
    slot_taken = slot_order[jnp.clip(position - CAP_T, 0, (blocks - 1) * CAP_T - 1)]
    other_block = slot_taken // CAP_T
    other_block = other_block + (other_block >= hot_block).astype(jnp.int32)
    chosen = jnp.where(position < CAP_T, hot_block, other_block)
    local_ids = jax.random.randint(key_local, (ROWS,), 0, ADP_T)
    return (chosen * ADP_T + local_ids).astype(jnp.int32)


def block_scale(rng, shape, cuts, least, top_value):
    loudness = 1.0
    for dim, blocks in cuts:
        draws = jax.random.uniform(jax.random.fold_in(jax.random.fold_in(rng, 6), dim), (blocks,), jnp.float32, least / len(cuts), top_value / len(cuts))
        loudness = loudness * jnp.repeat(jnp.exp(draws), shape[dim] // blocks).reshape((-1,) + (1,) * (len(shape) - 1 - dim))
    return loudness


def gaussian(own_key, dims, scale, limit, shards=(), kind=jnp.bfloat16):
    array = scale * jax.random.normal(own_key, dims, jnp.float32)
    if shards:
        array = array * block_scale(own_key, dims, shards, -0.22, 0.18)
    return jnp.clip(array, -limit, limit).astype(kind)


def setup_inputs(seed: int = 0) -> dict:
    arg_keys = jax.random.split(jax.random.key(seed), 9)
    return {
        "activations": gaussian(arg_keys[0], (STEPS, ROWS, D), 1.0, 6.0, ((1, 8), (2, 4))),
        "gate_weight": gaussian(arg_keys[1], (D, FF), D ** -0.5, 0.0625, ((0, 4), (1, 8))),
        "up_weight": gaussian(arg_keys[2], (D, FF), D ** -0.5, 0.0625, ((0, 4), (1, 8))),
        "down_weight": gaussian(arg_keys[3], (FF, D), FF ** -0.5, 0.03125, ((0, 8), (1, 4))),
        "shrink_weight": gaussian(arg_keys[4], (D, ADAPTERS * 2 * R), D ** -0.5, 0.0625, ((0, 4), (1, 8))),
        "expand_weight": gaussian(arg_keys[5], (2, ADAPTERS, R, FF), R ** -0.5, 1.5, ((1, 4), (3, 8))),
        "adapter_scale": jnp.clip(jnp.exp(math.log(2.0) - 1.3862944 * jax.random.uniform(arg_keys[6], (ADAPTERS,), jnp.float32) ** block_scale(arg_keys[6], (ADAPTERS,), ((0, 8),), -0.2, 0.2)), 0.5, 2.0),
        "adapter_ids": draw_adapter_ids(jax.random.fold_in(arg_keys[8], 71), 0),
    }


def reference(activations, gate_weight, up_weight, down_weight, shrink_weight, expand_weight, adapter_scale, adapter_ids):
    feat_width = D // N_TENSOR
    offsets = jnp.arange(ADP_T, dtype=jnp.int32)
    results = []
    for step_index in range(STEPS):
        tokens_now = activations[step_index]
        shrunk = jnp.dot(tokens_now, shrink_weight, preferred_element_type=jnp.float32).reshape(ROWS, ADAPTERS, 2 * R)
        picked = jnp.take_along_axis(shrunk, adapter_ids.astype(jnp.int32)[:, None, None], axis=1)[:, 0, :]
        low_inputs = (picked * adapter_scale[adapter_ids][:, None]).astype(jnp.bfloat16)
        gate_sum = jnp.zeros((ROWS, FF), jnp.float32)
        up_sum = jnp.zeros((ROWS, FF), jnp.float32)
        for block_index in range(N_TENSOR):
            member = (adapter_ids[:, None] == block_index * ADP_T + offsets[None, :]).astype(jnp.bfloat16)
            spread = jnp.repeat(member, R, axis=1)
            gate_low = jnp.tile(low_inputs[:, :R], (1, ADP_T)) * spread
            up_low = jnp.tile(low_inputs[:, R:], (1, ADP_T)) * spread
            first = block_index * feat_width
            slice_cols = tokens_now[:, first:first + feat_width]
            gate_expand = expand_weight[0, block_index * ADP_T:(block_index + 1) * ADP_T].reshape(ADP_T * R, FF)
            up_expand = expand_weight[1, block_index * ADP_T:(block_index + 1) * ADP_T].reshape(ADP_T * R, FF)
            gate_part = jnp.dot(slice_cols, gate_weight[first:first + feat_width], preferred_element_type=jnp.float32)
            gate_part = gate_part + jnp.dot(gate_low, gate_expand, preferred_element_type=jnp.float32)
            up_part = jnp.dot(slice_cols, up_weight[first:first + feat_width], preferred_element_type=jnp.float32)
            up_part = up_part + jnp.dot(up_low, up_expand, preferred_element_type=jnp.float32)
            gate_sum = gate_sum + lax.optimization_barrier(gate_part.astype(jnp.bfloat16)).astype(jnp.float32)
            up_sum = up_sum + lax.optimization_barrier(up_part.astype(jnp.bfloat16)).astype(jnp.float32)
        hidden = (jax.nn.silu(gate_sum) * up_sum).astype(jnp.bfloat16)
        results.append(jnp.dot(hidden, down_weight, preferred_element_type=jnp.float32).astype(jnp.bfloat16))
    return jnp.stack(results)
```

```python
import functools
import jax
import jax.numpy as jnp
from jax import lax
from jax.experimental import pallas as pl
from jax.experimental.pallas import tpu as pltpu
from jax.sharding import PartitionSpec as P

SHARES = (2, 3, 3, 3, 2, 1)
EARLY = 2
LIMIT = 16 * 1024 * 1024
PROJECT_LIMIT = 50 * 1024 * 1024


def transposed_dot(lows, maps):
    return lax.dot_general(lows, maps, (((0,), (0,)), ((), ())), preferred_element_type=jnp.float32)


def exact_dot(left, right):
    return jnp.dot(
        left, right, precision=lax.Precision.HIGHEST, preferred_element_type=jnp.float32
    )


def local_order(home, rows, entries, dp, dp_index):
    entry = lax.broadcasted_iota(jnp.int32, (entries, entries), 0)
    target = lax.broadcasted_iota(jnp.int32, (entries, entries), 1)
    local_row = entry % rows
    slot = local_row // home
    relative = jnp.where(slot < dp // 2, 2 * slot, 2 * slot - dp + 1)
    true_row = jnp.bitwise_xor(relative, dp_index) * home + local_row % home
    return (entry - local_row + true_row == target).astype(jnp.float32)


def shrink_kernel(home, dp, where_ref, scale_ref, x_ref, shrink_ref, ids_ref, *rest):
    out_ref = rest[-1]
    entries = x_ref.shape[0]
    wide = out_ref.shape[0]
    owner = where_ref[0]
    shrunk = lax.dot_general(
        shrink_ref[...], x_ref[...], (((0,), (1,)), ((), ())), preferred_element_type=jnp.float32
    )
    total = jnp.zeros(out_ref.shape, jnp.float32)
    order = local_order(home, home * dp, entries, dp, owner)
    ordered = exact_dot(shrunk, order)
    held = scale_ref.shape[0]
    for a in range(held):
        mine = jnp.where(ids_ref[...] == owner * held + a, scale_ref[a], 0.0)
        total = total + ordered[wide * a : wide * (a + 1)] * mine
    out_ref[...] = total


def lows_kernel(home, dp, count, rank, adapters, where_ref, ids_ref, *refs):
    low = refs[0][...]
    for ref in refs[1:count]:
        low = low + ref[...]
    out_ref = refs[-1]
    entries = low.shape[1]
    low = low.astype(jnp.bfloat16).astype(jnp.float32)
    order = local_order(home, home * dp, entries, dp, where_ref[0]).astype(jnp.bfloat16)
    depth = adapters * rank
    holder = lax.broadcasted_iota(jnp.int32, (depth, entries), 0) // rank
    for place in range(out_ref.shape[1] // depth):
        member = ids_ref[...] == where_ref[1 + place] * adapters + holder
        for j in range(2):
            tiled = jnp.concatenate([low[rank * j : rank * (j + 1)]] * adapters, axis=0)
            chosen = jnp.where(member, tiled, 0.0).astype(jnp.bfloat16)
            out_ref[j, depth * place : depth * (place + 1)] = lax.dot_general(
                chosen, order, (((1,), (1,)), ((), ())), preferred_element_type=jnp.float32
            ).astype(jnp.bfloat16)


def project_kernel(with_lows, x_ref, gate_ref, up_ref, *rest):
    out_ref = rest[-1]
    for j, weight_ref in enumerate((gate_ref, up_ref)):
        value = jnp.dot(x_ref[...], weight_ref[...], preferred_element_type=jnp.float32)
        if with_lows:
            depth = rest[1].shape[1]
            value = value + transposed_dot(rest[0][j, :depth], rest[1][j])
        out_ref[j] = value.astype(out_ref.dtype)


def fold_kernel(tile, first, maps, part_ref, got_ref, *rest):
    out_ref = rest[-1]
    for lo in range(0, out_ref.shape[2], tile):
        cols = slice(lo, lo + tile)
        for j in range(2):
            value = part_ref[j, :, cols].astype(jnp.float32) + got_ref[j, :, cols].astype(jnp.float32)
            for n in range(maps):
                depth = rest[1 + n].shape[1]
                value = value + transposed_dot(
                    rest[0][j, depth * n : depth * (n + 1)],
                    rest[1 + n][j, :, first + lo : first + lo + tile],
                )
            out_ref[j, :, cols] = value.astype(out_ref.dtype)


def hidden_kernel(tile, part_ref, *rest):
    out_ref = rest[-1]
    for lo in range(0, out_ref.shape[1], tile):
        cols = slice(lo, lo + tile)
        gate, up = part_ref[0, :, cols].astype(jnp.float32), part_ref[1, :, cols].astype(jnp.float32)
        if rest[0].shape == part_ref.shape:
            gate = gate + rest[0][0, :, cols].astype(jnp.float32)
            up = up + rest[0][1, :, cols].astype(jnp.float32)
        out_ref[:, cols] = (gate / (1.0 + jnp.exp(-gate)) * up).astype(out_ref.dtype)


def per_device(
    activations,
    gate_weight,
    up_weight,
    down_weight,
    shrink_weight,
    expand_weight,
    adapter_scale,
    adapter_ids,
):
    f32, bf16 = jnp.float32, jnp.bfloat16
    dp, tp = lax.axis_size("dp"), lax.axis_size("tensor")
    dp_index, tp_index = lax.axis_index("dp"), lax.axis_index("tensor")
    steps, home, feat = activations.shape
    rows = home * dp
    entries = steps * rows
    adp_block, low_rank, ff_local = expand_weight.shape[1:]
    depth = adp_block * low_rank
    out_feat = down_weight.shape[1]
    left = tp_index < tp // 2
    number = lambda value: jnp.asarray(value, jnp.int32).reshape(1)
    inner = tp // 2
    tile = 256 if ff_local % 256 == 0 else 128

    def dp_xor(value, k):
        return lax.ppermute(value, "dp", [(s, s ^ k) for s in range(dp)])

    def tp_send(value, pairs):
        return lax.ppermute(value, "tensor", pairs)

    def gated(value, *others):
        return lax.optimization_barrier((value,) + others)[0] if others else value

    groups, done, bounds = ff_local // tile, 0, [0]
    for share in SHARES:
        done += share
        bounds.append(groups * done // sum(SHARES) * tile)
    spans = [(lo, hi) for lo, hi in zip(bounds[:-1], bounds[1:]) if hi > lo]
    widths = [hi - lo for lo, hi in spans]
    count = len(spans)
    fold = [[(s, s + 1), (tp - 1 - s, tp - 2 - s)] for s in range(inner - 1)]
    across = [(inner - 1, inner), (inner, inner - 1)]
    unfold = [[(inner - 1 - s, inner - 2 - s), (inner + s, inner + s + 1)] for s in range(inner - 1)]

    params = pltpu.CompilerParams(vmem_limit_bytes=LIMIT)
    scalar = pl.BlockSpec(memory_space=pltpu.SMEM)
    anywhere = pl.BlockSpec(memory_space=pl.ANY)

    def whole(value):
        return pl.BlockSpec(value.shape, lambda *t: (0,) * value.ndim)

    def cost(flops, nbytes):
        return pl.CostEstimate(flops=1, bytes_accessed=1, transcendentals=0)

    even = [activations] + [dp_xor(activations, k) for k in range(2, dp, 2)]
    odd = [dp_xor(value, 1) for value in even]
    x_all = jnp.concatenate(even + odd, axis=1).reshape(entries, feat)

    expand = expand_weight.reshape(2, depth, ff_local)
    early = min(EARLY, count - 1)
    maps = [expand[:, :, : spans[early - 1][1]]]
    maps.append(tp_send(maps[0], fold[0]))
    blocks = [tp_index, jnp.where(left, tp_index - 1, tp_index + 1)]

    def project(c, *after):
        lo, hi = spans[c]
        wide = 2 * tile if lo % (2 * tile) == 0 and hi % (2 * tile) == 0 else tile
        first = lo // wide
        weights = pl.BlockSpec((feat, wide), lambda t: (0, first + t))
        operands, specs = [x_all, gate_weight, up_weight], [whole(x_all), weights, weights]
        if c >= early:
            operands += [lows, expand]
            specs += [whole(lows), pl.BlockSpec((2, depth, wide), lambda t: (0, 0, first + t))]
        return pl.pallas_call(
            functools.partial(project_kernel, c >= early),
            grid=((hi - lo) // wide,),
            in_specs=specs + [anywhere] * len(after),
            out_specs=pl.BlockSpec((2, entries, wide), lambda t: (0, 0, t)),
            out_shape=jax.ShapeDtypeStruct((2, entries, hi - lo), bf16),
            compiler_params=pltpu.CompilerParams(vmem_limit_bytes=PROJECT_LIMIT),
            cost_estimate=cost(4 * entries * feat * (hi - lo), 8 * feat * (hi - lo)),
            name="project",
        )(*operands, *after)

    global_ids = jnp.tile(adapter_ids, (steps,)).reshape(1, entries)
    partial = pl.pallas_call(
        functools.partial(shrink_kernel, home, dp),
        in_specs=[scalar, scalar, whole(x_all), whole(shrink_weight), whole(global_ids)],
        out_specs=pl.BlockSpec((2 * low_rank, entries), lambda: (0, 0)),
        out_shape=jax.ShapeDtypeStruct((2 * low_rank, entries), f32),
        compiler_params=params,
        cost_estimate=cost(2**27, 2**21),
        name="shrink",
    )(number(dp_index), adapter_scale, x_all, shrink_weight, global_ids)
    low = functools.reduce(
        jnp.add, [partial] + [tp_send(partial, [(s, s ^ k) for s in range(tp)]) for k in range(1, tp)]
    )
    parts = {0: project(0, low)}
    first_got = {0: tp_send(parts[0], fold[0])}
    low = functools.reduce(
        jnp.add, [gated(low, parts[0])] + [dp_xor(low, k) for k in range(2, dp, 2)]
    )
    for c in range(1, early):
        parts[c] = project(c, low, maps[1])
        first_got[c] = tp_send(parts[c], fold[0])
    pieces = [low, dp_xor(low, 1)]
    lows = pl.pallas_call(
        functools.partial(lows_kernel, home, dp, len(pieces), low_rank, adp_block),
        in_specs=[scalar, whole(global_ids)] + [whole(low)] * len(pieces),
        out_specs=pl.BlockSpec((2, len(blocks) * depth, entries), lambda: (0, 0, 0)),
        out_shape=jax.ShapeDtypeStruct((2, len(blocks) * depth, entries), bf16),
        compiler_params=params,
        cost_estimate=cost(2**27, 2**20),
        name="lows",
    )(
        jnp.concatenate([number(dp_index)] + [number(block) for block in blocks]), global_ids, *pieces
    )

    def small(kernel, name, shape, operands, *after):
        return pl.pallas_call(
            kernel,
            in_specs=[whole(value) for value in operands] + [anywhere] * len(after),
            out_specs=pl.BlockSpec(shape, lambda: (0,) * len(shape)),
            out_shape=jax.ShapeDtypeStruct(shape, bf16),
            compiler_params=params,
            cost_estimate=cost(2**24, 2**22),
            name=name,
        )(*operands, *after)

    folded, cross_got, hiddens, full_got = {}, {}, {}, {}

    def stage_fold(c, *after):
        part = parts[c]
        for s, pairs in enumerate(fold):
            got = first_got[c] if s == 0 else tp_send(part, pairs)
            extra = [lows] + maps if c < early and s == 0 else []
            part = small(
                functools.partial(fold_kernel, tile, spans[c][0], len(extra[1:])),
                "fold",
                part.shape,
                [part, got] + extra,
                *after,
            )
        folded[c] = part
        cross_got[c] = tp_send(part, across)

    def stage_hidden(c, *after):
        hidden = small(
            functools.partial(hidden_kernel, tile),
            "hidden",
            (entries, widths[c]),
            [folded[c], cross_got[c]],
            *after,
        )
        hiddens[c] = hidden
        for s, pairs in enumerate(unfold):
            got = tp_send(hidden, pairs)
            if s < len(unfold) - 1:
                fresh = (tp_index == inner - 2 - s) | (tp_index == inner + s + 1)
                hidden = jnp.where(fresh, got, hidden)
        full_got[c] = (hidden, got)

    def down(c, hidden, total, *after):
        value = jnp.dot(gated(hidden, *after), down_weight[slice(*spans[c])], preferred_element_type=f32)
        return value if total is None else total + value

    outermost = (tp_index == 0) | (tp_index == tp - 1)

    def stage_down(c, total, *after):
        hidden, got = full_got[c]
        return down(c, jnp.where(outermost, gated(got, *after), hidden), total)

    latest, total = [], None
    for t in range(count + 2):
        if t < count:
            stage_fold(t, *latest)
            latest = [folded[t]]
        if t + 2 < count:
            if t == 0:
                parts[2] = project(2, folded[0])
                latest = [parts[2]]
            first_got[t + 2] = tp_send(gated(parts[t + 2], folded[t]), fold[0])
        if t + 3 < count:
            parts[t + 3] = project(t + 3, *latest)
            latest = [parts[t + 3]]
        for c in (t - 1, t):
            ahead = c + 1 < count and widths[c + 1] > widths[c]
            if 0 <= c < count and ahead == (c == t):
                stage_hidden(c, *latest)
                latest = [hiddens[c]]
        if t >= 2:
            total = stage_down(t - 2, total, *latest)
            latest = [total]

    total = total.reshape(steps, rows, out_feat)
    got = dp_xor(total[:, rows // 2 :].astype(bf16), 1)
    pair = total[:, : rows // 2] + got.astype(f32)
    pair_sent = pair.astype(bf16)
    mixed = pair[:, :home]
    for e in range(1, dp // 2):
        mixed = mixed + dp_xor(pair_sent[:, e * home : (e + 1) * home], 2 * e).astype(f32)
    mixed = mixed.astype(bf16)
    return mixed


def solution(mesh):
    placed = (
        P(None, "dp", "tensor"),
        P("tensor", "dp"),
        P("tensor", "dp"),
        P("dp", "tensor"),
        P("tensor", "dp"),
        P(None, "tensor", None, "dp"),
        P("dp"),
        P(),
    )
    return jax.shard_map(
        per_device, mesh=mesh, in_specs=placed, out_specs=P(None, "dp", "tensor"), check_vma=False
    )
```

```python
import functools
import jax
import jax.numpy as jnp
from jax import lax
from jax.experimental import pallas as pl
from jax.experimental.pallas import tpu as pltpu
from jax.sharding import PartitionSpec as P

SHARES = (1, 2, 3, 3, 3, 2)
GROUPS = (1, 1, 1, 1, 1, 1, 1)
AHEAD = (1, 1, 0, 0, 0)
EARLY = 2
LIMIT = 24 * 1024 * 1024
PROJECT_LIMIT = 50 * 1024 * 1024


def transposed_dot(lows, maps):
    return lax.dot_general(lows, maps, (((0,), (0,)), ((), ())), preferred_element_type=jnp.float32)


def exact_dot(left, right):
    return jnp.dot(
        left, right, precision=lax.Precision.HIGHEST, preferred_element_type=jnp.float32
    )


def local_order(home, rows, entries, dp, dp_index):
    entry = lax.broadcasted_iota(jnp.int32, (entries, entries), 0)
    target = lax.broadcasted_iota(jnp.int32, (entries, entries), 1)
    local_row = entry % rows
    slot = local_row // home
    relative = jnp.where(slot < dp // 2, 2 * slot, 2 * slot - dp + 1)
    true_row = jnp.bitwise_xor(relative, dp_index) * home + local_row % home
    return (entry - local_row + true_row == target).astype(jnp.float32)


def shrink_kernel(home, dp, where_ref, scale_ref, x_ref, shrink_ref, ids_ref, *rest):
    out_ref = rest[-1]
    entries = x_ref.shape[0]
    wide = out_ref.shape[0]
    owner = where_ref[0]
    shrunk = lax.dot_general(
        shrink_ref[...], x_ref[...], (((0,), (1,)), ((), ())), preferred_element_type=jnp.float32
    )
    total = jnp.zeros(out_ref.shape, jnp.float32)
    order = local_order(home, home * dp, entries, dp, owner)
    ordered = exact_dot(shrunk, order)
    held = scale_ref.shape[0]
    for a in range(held):
        mine = jnp.where(ids_ref[...] == owner * held + a, scale_ref[a], 0.0)
        total = total + ordered[wide * a : wide * (a + 1)] * mine
    out_ref[...] = total


def lows_kernel(home, dp, count, rank, adapters, where_ref, ids_ref, *refs):
    low = refs[0][...]
    for ref in refs[1:count]:
        low = low + ref[...]
    out_ref = refs[-1]
    entries = low.shape[1]
    low = low.astype(jnp.bfloat16).astype(jnp.float32)
    order = local_order(home, home * dp, entries, dp, where_ref[0]).astype(jnp.bfloat16)
    depth = adapters * rank
    holder = lax.broadcasted_iota(jnp.int32, (depth, entries), 0) // rank
    for place in range(2):
        member = ids_ref[...] == where_ref[1 + place] * adapters + holder
        for j in range(2):
            tiled = jnp.concatenate([low[rank * j : rank * (j + 1)]] * adapters, axis=0)
            chosen = jnp.where(member, tiled, 0.0).astype(jnp.bfloat16)
            out_ref[j, depth * place : depth * (place + 1)] = lax.dot_general(
                chosen, order, (((1,), (1,)), ((), ())), preferred_element_type=jnp.float32
            ).astype(jnp.bfloat16)


def project_kernel(with_lows, x_ref, gate_ref, up_ref, *rest):
    out_ref = rest[-1]
    for j, weight_ref in enumerate((gate_ref, up_ref)):
        value = jnp.dot(x_ref[...], weight_ref[...], preferred_element_type=jnp.float32)
        if with_lows:
            depth = rest[1].shape[1]
            value = value + transposed_dot(rest[0][j, :depth], rest[1][j])
        out_ref[j] = value.astype(out_ref.dtype)


def fold_kernel(tile, first, maps, outputs, part_ref, got_ref, *rest):
    out_ref = rest[len(rest) - outputs]
    for lo in range(0, out_ref.shape[2], tile):
        cols = slice(lo, lo + tile)
        for j in range(2):
            value = part_ref[j, :, cols].astype(jnp.float32) + got_ref[j, :, cols].astype(jnp.float32)
            for n in range(maps):
                depth = rest[1 + n].shape[1]
                value = value + transposed_dot(
                    rest[0][j, depth * n : depth * (n + 1)],
                    rest[1 + n][j, :, first + lo : first + lo + tile],
                )
            out_ref[j, :, cols] = value.astype(out_ref.dtype)


def hidden_kernel(tile, earlier, part_ref, *rest):
    out_ref = rest[-1]
    first = 0
    for ref in rest[1 : 1 + earlier]:
        width = ref.shape[1]
        out_ref[:, first : first + width] = ref[...]
        first += width
    for lo in range(0, part_ref.shape[2], tile):
        cols = slice(lo, lo + tile)
        gate, up = part_ref[0, :, cols].astype(jnp.float32), part_ref[1, :, cols].astype(jnp.float32)
        if rest[0].shape == part_ref.shape:
            gate = gate + rest[0][0, :, cols].astype(jnp.float32)
            up = up + rest[0][1, :, cols].astype(jnp.float32)
        place = slice(first + lo, first + lo + tile)
        out_ref[:, place] = (gate / (1.0 + jnp.exp(-gate)) * up).astype(out_ref.dtype)


def per_device(
    activations,
    gate_weight,
    up_weight,
    down_weight,
    shrink_weight,
    expand_weight,
    adapter_scale,
    adapter_ids,
):
    f32, bf16 = jnp.float32, jnp.bfloat16
    dp, tp = lax.axis_size("dp"), lax.axis_size("tensor")
    dp_index, tp_index = lax.axis_index("dp"), lax.axis_index("tensor")
    steps, home, feat = activations.shape
    rows = home * dp
    entries = steps * rows
    adp_block, low_rank, ff_local = expand_weight.shape[1:]
    depth = adp_block * low_rank
    out_feat = down_weight.shape[1]
    number = lambda value: jnp.asarray(value, jnp.int32).reshape(1)
    inner = tp // 2
    tile = 256 if ff_local % 256 == 0 else 128

    def dp_xor(value, k):
        return lax.ppermute(value, "dp", [(s, s ^ k) for s in range(dp)])

    def tp_send(value, pairs):
        return lax.ppermute(value, "tensor", pairs)

    def gated(value, *others):
        return lax.optimization_barrier((value,) + others)[0] if others else value

    groups, done, bounds = ff_local // tile, 0, [0]
    for share in SHARES:
        done += share
        bounds.append(groups * done // sum(SHARES) * tile)
    spans = [(lo, hi) for lo, hi in zip(bounds[:-1], bounds[1:]) if hi > lo]
    widths = [hi - lo for lo, hi in spans]
    count = len(spans)
    fold = [[(s, s + 1), (tp - 1 - s, tp - 2 - s)] for s in range(inner - 1)]
    across = [(inner - 1, inner), (inner, inner - 1)]
    unfold = [[(inner - 1 - s, inner - 2 - s), (inner + s, inner + s + 1)] for s in range(inner - 1)]

    params = pltpu.CompilerParams(vmem_limit_bytes=LIMIT)
    scalar = pl.BlockSpec(memory_space=pltpu.SMEM)
    anywhere = pl.BlockSpec(memory_space=pl.ANY)

    def whole(value):
        return pl.BlockSpec(value.shape, lambda *t: (0,) * value.ndim)

    def cost(flops, nbytes):
        return pl.CostEstimate(flops=1, bytes_accessed=1, transcendentals=0)

    even = [activations] + [dp_xor(activations, k) for k in range(2, dp, 2)]
    odd = [dp_xor(value, 1) for value in even]
    x_all = jnp.concatenate(even + odd, axis=1).reshape(entries, feat)

    expand = expand_weight.reshape(2, depth, ff_local)
    early = min(EARLY, count - 1)
    maps = [expand[:, :, : spans[early - 1][1]]]
    maps.append(tp_send(maps[0], fold[0]))
    away = jnp.where(tp_index < inner, tp_index - 1, tp_index + 1)

    def project(c, *after):
        lo, hi = spans[c]
        wide = 2 * tile if lo % (2 * tile) == 0 and hi % (2 * tile) == 0 else tile
        first = lo // wide
        weights = pl.BlockSpec((feat, wide), lambda t: (0, first + t))
        operands, specs = [x_all, gate_weight, up_weight], [whole(x_all), weights, weights]
        if c >= early:
            operands += [lows, expand]
            specs += [whole(lows), pl.BlockSpec((2, depth, wide), lambda t: (0, 0, first + t))]
        return pl.pallas_call(
            functools.partial(project_kernel, c >= early),
            grid=((hi - lo) // wide,),
            in_specs=specs + [anywhere] * len(after),
            out_specs=pl.BlockSpec((2, entries, wide), lambda t: (0, 0, t)),
            out_shape=jax.ShapeDtypeStruct((2, entries, hi - lo), bf16),
            compiler_params=pltpu.CompilerParams(vmem_limit_bytes=PROJECT_LIMIT),
            cost_estimate=cost(4 * entries * feat * (hi - lo), 8 * feat * (hi - lo)),
            name="project",
        )(*operands, *after)

    global_ids = jnp.tile(adapter_ids, (steps,)).reshape(1, entries)
    partial = pl.pallas_call(
        functools.partial(shrink_kernel, home, dp),
        in_specs=[scalar, scalar, whole(x_all), whole(shrink_weight), whole(global_ids), anywhere],
        out_specs=pl.BlockSpec((2 * low_rank, entries), lambda: (0, 0)),
        out_shape=jax.ShapeDtypeStruct((2 * low_rank, entries), f32),
        compiler_params=params,
        cost_estimate=cost(2**27, 2**21),
        name="shrink",
    )(number(dp_index), adapter_scale, x_all, shrink_weight, global_ids, global_ids)
    parts = {0: project(0, partial)}
    first_got = {0: tp_send(parts[0], fold[0])}
    low = functools.reduce(
        jnp.add, [gated(partial, parts[0])] + [tp_send(partial, [(s, s ^ k) for s in range(tp)]) for k in range(1, tp)]
    )
    for c in range(1, early):
        parts[c] = project(c, low)
        first_got[c] = tp_send(parts[c], fold[0])
    low = functools.reduce(
        jnp.add, [gated(low, parts[early - 1])] + [dp_xor(low, k) for k in range(2, dp, 2)]
    )
    pieces = [low, dp_xor(low, 1)]
    lows = pl.pallas_call(
        functools.partial(lows_kernel, home, dp, len(pieces), low_rank, adp_block),
        in_specs=[scalar, whole(global_ids)] + [whole(low)] * len(pieces),
        out_specs=pl.BlockSpec((2, 2 * depth, entries), lambda: (0, 0, 0)),
        out_shape=jax.ShapeDtypeStruct((2, 2 * depth, entries), bf16),
        compiler_params=params,
        cost_estimate=cost(2**27, 2**20),
        name="lows",
    )(
        jnp.concatenate([number(dp_index), number(tp_index), number(away)]), global_ids, *pieces
    )

    def small(kernel, name, shape, operands, *after):
        return pl.pallas_call(
            kernel,
            in_specs=[whole(value) for value in operands] + [anywhere] * len(after),
            out_specs=pl.BlockSpec(shape, lambda: (0,) * len(shape)),
            out_shape=jax.ShapeDtypeStruct(shape, bf16),
            compiler_params=params,
            cost_estimate=cost(2**24, 2**22),
            name=name,
        )(*operands, *after)

    def fold_call(c, part, got, ahead, *after):
        shapes = [jax.ShapeDtypeStruct(part.shape, bf16)]
        operands = [part, got]
        specs = [whole(part), whole(got)]
        outs = [pl.BlockSpec(part.shape, lambda: (0,) * part.ndim)]
        extra = [lows] + maps if c < early else []
        operands += extra
        specs += [whole(value) for value in extra]
        if ahead is not None:
            operands.append(ahead)
            specs.append(anywhere)
            outs.append(anywhere)
            shapes.append(jax.ShapeDtypeStruct(ahead.shape, bf16))
        result = pl.pallas_call(
            functools.partial(
                fold_kernel, tile, spans[c][0] if extra else 0, len(extra[1:]), len(outs)
            ),
            in_specs=specs + [anywhere] * len(after),
            out_specs=outs,
            out_shape=shapes,
            input_output_aliases={2 + len(extra): 1} if ahead is not None else {},
            compiler_params=params,
            cost_estimate=cost(2**24, 2**22),
            name="fold",
        )(*operands, *after)
        return result if ahead is not None else (result[0], None)

    folded, cross_got, hiddens, full_got = {}, {}, {}, {}

    def stage_fold(c, *after):
        part = parts[c]
        for s, pairs in enumerate(fold):
            got = first_got[c] if s == 0 else tp_send(part, pairs)
            ahead = parts.get(c + 2) if s == 0 and c + 2 not in first_got else None
            part, ahead = fold_call(c if s == 0 else count, part, got, ahead, *after)
            if ahead is not None:
                parts[c + 2] = ahead
        folded[c] = part
        cross_got[c] = tp_send(part, across)

    ends, first = {}, 0
    for size in GROUPS:
        last = min(first + size, count) - 1
        if last >= first:
            ends[last] = first
        first = last + 1
    if count - 1 not in ends:
        ends[count - 1] = first

    def stage_hidden(c, *after):
        earlier = list(range(ends[c], c)) if c in ends else []
        width = sum(widths[n] for n in earlier + [c])
        hidden = small(
            functools.partial(hidden_kernel, tile, len(earlier)),
            "hidden",
            (entries, width),
            [folded[c], cross_got[c]] + [hiddens[n] for n in earlier],
            *after,
        )
        hiddens[c] = hidden
        if c not in ends:
            return
        for s, pairs in enumerate(unfold):
            got = tp_send(hidden, pairs)
            if s < len(unfold) - 1:
                fresh = (tp_index == inner - 2 - s) | (tp_index == inner + s + 1)
                hidden = jnp.where(fresh, got, hidden)
        full_got[c] = (hidden, got)

    outermost = (tp_index == 0) | (tp_index == tp - 1)

    def stage_down(c, total, *after):
        hidden, got = full_got[c]
        hidden = gated(jnp.where(outermost, got, hidden), *after)
        rows_of = slice(spans[ends[c]][0], spans[c][1])
        value = jnp.dot(hidden, down_weight[rows_of], preferred_element_type=f32)
        return value if total is None else total + value

    latest, total = [], None
    for t in range(count + 2):
        if t < count:
            stage_fold(t, *latest)
            latest = [folded[t]]
        if t + 2 < count:
            parts[t + 2] = project(t + 2, *latest)
            latest = [parts[t + 2]]
            first_got[t + 2] = tp_send(parts[t + 2], fold[0])
        for c in (t - 1, t):
            ahead = c + 1 < count and bool(AHEAD[c])
            if 0 <= c < count and ahead == (c == t):
                stage_hidden(c, *latest)
                latest = [hiddens[c]]
        if t - 2 in ends:
            total = stage_down(t - 2, total, *latest)
            latest = [total]

    total = total.reshape(steps, rows, out_feat)
    got = dp_xor(total[:, rows // 2 :].astype(bf16), 1)
    pair = total[:, : rows // 2] + got.astype(f32)
    pair_sent = pair.astype(bf16)
    mixed = pair[:, :home]
    for e in range(1, dp // 2):
        mixed = mixed + dp_xor(pair_sent[:, e * home : (e + 1) * home], 2 * e).astype(f32)
    mixed = mixed.astype(bf16)
    return mixed


def solution(mesh):
    placed = (
        P(None, "dp", "tensor"),
        P("tensor", "dp"),
        P("tensor", "dp"),
        P("dp", "tensor"),
        P("tensor", "dp"),
        P(None, "tensor", None, "dp"),
        P("dp"),
        P(),
    )
    return jax.shard_map(
        per_device, mesh=mesh, in_specs=placed, out_specs=P(None, "dp", "tensor"), check_vma=False
    )
```

```python
import functools
import jax
import jax.numpy as jnp
from jax import lax
from jax.experimental import pallas as pl
from jax.experimental.pallas import tpu as pltpu
from jax.sharding import PartitionSpec as P

SHARES = (1, 2, 3, 3, 3, 2)
GROUPS = (1, 1, 1, 1, 1, 1, 1)
AHEAD = (1, 1, 0, 0, 0)
EARLY = 2
LIMIT = 24 * 1024 * 1024
PROJECT_LIMIT = 50 * 1024 * 1024


def transposed_dot(lows, maps):
    return lax.dot_general(lows, maps, (((0,), (0,)), ((), ())), preferred_element_type=jnp.float32)


def exact_dot(left, right):
    return jnp.dot(
        left, right, precision=lax.Precision.HIGHEST, preferred_element_type=jnp.float32
    )


def local_order(home, rows, entries, dp, dp_index):
    entry = lax.broadcasted_iota(jnp.int32, (entries, entries), 0)
    target = lax.broadcasted_iota(jnp.int32, (entries, entries), 1)
    local_row = entry % rows
    slot = local_row // home
    relative = jnp.where(slot < dp // 2, 2 * slot, 2 * slot - dp + 1)
    true_row = jnp.bitwise_xor(relative, dp_index) * home + local_row % home
    return (entry - local_row + true_row == target).astype(jnp.float32)


def shrink_kernel(home, dp, where_ref, scale_ref, x_ref, shrink_ref, ids_ref, *rest):
    out_ref = rest[-1]
    entries = x_ref.shape[0]
    wide = out_ref.shape[0]
    owner = where_ref[0]
    shrunk = lax.dot_general(
        shrink_ref[...], x_ref[...], (((0,), (1,)), ((), ())), preferred_element_type=jnp.float32
    )
    total = jnp.zeros(out_ref.shape, jnp.float32)
    order = local_order(home, home * dp, entries, dp, owner)
    ordered = exact_dot(shrunk, order)
    held = scale_ref.shape[0]
    for a in range(held):
        mine = jnp.where(ids_ref[...] == owner * held + a, scale_ref[a], 0.0)
        total = total + ordered[wide * a : wide * (a + 1)] * mine
    out_ref[...] = total


def lows_kernel(home, dp, count, rank, adapters, where_ref, ids_ref, *refs):
    low = refs[0][...]
    for ref in refs[1:count]:
        low = low + ref[...]
    out_ref = refs[-1]
    entries = low.shape[1]
    low = low.astype(jnp.bfloat16).astype(jnp.float32)
    order = local_order(home, home * dp, entries, dp, where_ref[0]).astype(jnp.bfloat16)
    depth = adapters * rank
    holder = lax.broadcasted_iota(jnp.int32, (depth, entries), 0) // rank
    for place in range(2):
        member = ids_ref[...] == where_ref[1 + place] * adapters + holder
        for j in range(2):
            tiled = jnp.concatenate([low[rank * j : rank * (j + 1)]] * adapters, axis=0)
            chosen = jnp.where(member, tiled, 0.0).astype(jnp.bfloat16)
            out_ref[j, depth * place : depth * (place + 1)] = lax.dot_general(
                chosen, order, (((1,), (1,)), ((), ())), preferred_element_type=jnp.float32
            ).astype(jnp.bfloat16)


def project_kernel(with_lows, x_ref, gate_ref, up_ref, *rest):
    out_ref = rest[-1]
    for j, weight_ref in enumerate((gate_ref, up_ref)):
        value = jnp.dot(x_ref[...], weight_ref[...], preferred_element_type=jnp.float32)
        if with_lows:
            depth = rest[1].shape[1]
            value = value + transposed_dot(rest[0][j, :depth], rest[1][j])
        out_ref[j] = value.astype(out_ref.dtype)


def fold_kernel(tile, first, maps, outputs, part_ref, got_ref, *rest):
    out_ref = rest[len(rest) - outputs]
    for lo in range(0, out_ref.shape[2], tile):
        cols = slice(lo, lo + tile)
        for j in range(2):
            value = part_ref[j, :, cols].astype(jnp.float32) + got_ref[j, :, cols].astype(jnp.float32)
            for n in range(maps):
                depth = rest[1 + n].shape[1]
                value = value + transposed_dot(
                    rest[0][j, depth * n : depth * (n + 1)],
                    rest[1 + n][j, :, first + lo : first + lo + tile],
                )
            out_ref[j, :, cols] = value.astype(out_ref.dtype)


def hidden_kernel(tile, earlier, part_ref, *rest):
    out_ref = rest[-1]
    first = 0
    for ref in rest[1 : 1 + earlier]:
        width = ref.shape[1]
        out_ref[:, first : first + width] = ref[...]
        first += width
    for lo in range(0, part_ref.shape[2], tile):
        cols = slice(lo, lo + tile)
        gate, up = part_ref[0, :, cols].astype(jnp.float32), part_ref[1, :, cols].astype(jnp.float32)
        if rest[0].shape == part_ref.shape:
            gate = gate + rest[0][0, :, cols].astype(jnp.float32)
            up = up + rest[0][1, :, cols].astype(jnp.float32)
        place = slice(first + lo, first + lo + tile)
        out_ref[:, place] = (gate / (1.0 + jnp.exp(-gate)) * up).astype(out_ref.dtype)


def per_device(
    activations,
    gate_weight,
    up_weight,
    down_weight,
    shrink_weight,
    expand_weight,
    adapter_scale,
    adapter_ids,
):
    f32, bf16 = jnp.float32, jnp.bfloat16
    dp, tp = lax.axis_size("dp"), lax.axis_size("tensor")
    dp_index, tp_index = lax.axis_index("dp"), lax.axis_index("tensor")
    steps, home, feat = activations.shape
    rows = home * dp
    entries = steps * rows
    adp_block, low_rank, ff_local = expand_weight.shape[1:]
    depth = adp_block * low_rank
    out_feat = down_weight.shape[1]
    number = lambda value: jnp.asarray(value, jnp.int32).reshape(1)
    inner = tp // 2
    tile = 256 if ff_local % 256 == 0 else 128

    def dp_xor(value, k):
        return lax.ppermute(value, "dp", [(s, s ^ k) for s in range(dp)])

    def tp_send(value, pairs):
        return lax.ppermute(value, "tensor", pairs)

    def gated(value, *others):
        return lax.optimization_barrier((value,) + others)[0] if others else value

    groups, done, bounds = ff_local // tile, 0, [0]
    for share in SHARES:
        done += share
        bounds.append(groups * done // sum(SHARES) * tile)
    spans = [(lo, hi) for lo, hi in zip(bounds[:-1], bounds[1:]) if hi > lo]
    widths = [hi - lo for lo, hi in spans]
    count = len(spans)
    fold = [[(s, s + 1), (tp - 1 - s, tp - 2 - s)] for s in range(inner - 1)]
    across = [(inner - 1, inner), (inner, inner - 1)]
    unfold = [[(inner - 1 - s, inner - 2 - s), (inner + s, inner + s + 1)] for s in range(inner - 1)]

    params = pltpu.CompilerParams(vmem_limit_bytes=LIMIT)
    scalar = pl.BlockSpec(memory_space=pltpu.SMEM)
    anywhere = pl.BlockSpec(memory_space=pl.ANY)

    def whole(value):
        return pl.BlockSpec(value.shape, lambda *t: (0,) * value.ndim)

    def cost(flops, nbytes):
        return pl.CostEstimate(flops=1, bytes_accessed=1, transcendentals=0)

    even = [activations] + [dp_xor(activations, k) for k in range(2, dp, 2)]
    odd = [dp_xor(value, 1) for value in even]
    x_all = jnp.concatenate(even + odd, axis=1).reshape(entries, feat)

    expand = expand_weight.reshape(2, depth, ff_local)
    early = min(EARLY, count - 1)
    maps = [expand[:, :, : spans[early - 1][1]]]
    maps.append(tp_send(maps[0], fold[0]))
    away = jnp.where(tp_index < inner, tp_index - 1, tp_index + 1)

    def project(c, *after):
        lo, hi = spans[c]
        wide = 2 * tile if lo % (2 * tile) == 0 and hi % (2 * tile) == 0 else tile
        first = lo // wide
        weights = pl.BlockSpec((feat, wide), lambda t: (0, first + t))
        operands, specs = [x_all, gate_weight, up_weight], [whole(x_all), weights, weights]
        if c >= early:
            operands += [lows, expand]
            specs += [whole(lows), pl.BlockSpec((2, depth, wide), lambda t: (0, 0, first + t))]
        return pl.pallas_call(
            functools.partial(project_kernel, c >= early),
            grid=((hi - lo) // wide,),
            in_specs=specs + [anywhere] * len(after),
            out_specs=pl.BlockSpec((2, entries, wide), lambda t: (0, 0, t)),
            out_shape=jax.ShapeDtypeStruct((2, entries, hi - lo), bf16),
            compiler_params=pltpu.CompilerParams(vmem_limit_bytes=PROJECT_LIMIT),
            cost_estimate=cost(4 * entries * feat * (hi - lo), 8 * feat * (hi - lo)),
            name="project",
        )(*operands, *after)

    global_ids = jnp.tile(adapter_ids, (steps,)).reshape(1, entries)
    partial = pl.pallas_call(
        functools.partial(shrink_kernel, home, dp),
        in_specs=[scalar, scalar, whole(x_all), whole(shrink_weight), whole(global_ids), anywhere],
        out_specs=pl.BlockSpec((2 * low_rank, entries), lambda: (0, 0)),
        out_shape=jax.ShapeDtypeStruct((2 * low_rank, entries), f32),
        compiler_params=params,
        cost_estimate=cost(2**27, 2**21),
        name="shrink",
    )(number(dp_index), adapter_scale, x_all, shrink_weight, global_ids, global_ids)
    parts = {0: project(0, partial)}
    first_got = {0: tp_send(parts[0], fold[0])}
    low = functools.reduce(
        jnp.add, [gated(partial, parts[0])] + [tp_send(partial, [(s, s ^ k) for s in range(tp)]) for k in range(1, tp)]
    )
    for c in range(1, early):
        parts[c] = project(c, low, maps[1])
        first_got[c] = tp_send(parts[c], fold[0])
    low = functools.reduce(
        jnp.add, [gated(low, parts[early - 1])] + [dp_xor(low, k) for k in range(2, dp, 2)]
    )
    pieces = [low, dp_xor(low, 1)]
    lows = pl.pallas_call(
        functools.partial(lows_kernel, home, dp, len(pieces), low_rank, adp_block),
        in_specs=[scalar, whole(global_ids)] + [whole(low)] * len(pieces),
        out_specs=pl.BlockSpec((2, 2 * depth, entries), lambda: (0, 0, 0)),
        out_shape=jax.ShapeDtypeStruct((2, 2 * depth, entries), bf16),
        compiler_params=params,
        cost_estimate=cost(2**27, 2**20),
        name="lows",
    )(
        jnp.concatenate([number(dp_index), number(tp_index), number(away)]), global_ids, *pieces
    )

    def small(kernel, name, shape, operands, *after):
        return pl.pallas_call(
            kernel,
            in_specs=[whole(value) for value in operands] + [anywhere] * len(after),
            out_specs=pl.BlockSpec(shape, lambda: (0,) * len(shape)),
            out_shape=jax.ShapeDtypeStruct(shape, bf16),
            compiler_params=params,
            cost_estimate=cost(2**24, 2**22),
            name=name,
        )(*operands, *after)

    def fold_call(c, part, got, ahead, *after):
        shapes = [jax.ShapeDtypeStruct(part.shape, bf16)]
        operands = [part, got]
        specs = [whole(part), whole(got)]
        outs = [pl.BlockSpec(part.shape, lambda: (0,) * part.ndim)]
        extra = [lows] + maps if c < early else []
        operands += extra
        specs += [whole(value) for value in extra]
        if ahead is not None:
            operands.append(ahead)
            specs.append(anywhere)
            outs.append(anywhere)
            shapes.append(jax.ShapeDtypeStruct(ahead.shape, bf16))
        result = pl.pallas_call(
            functools.partial(
                fold_kernel, tile, spans[c][0] if extra else 0, len(extra[1:]), len(outs)
            ),
            in_specs=specs + [anywhere] * len(after),
            out_specs=outs,
            out_shape=shapes,
            input_output_aliases={2 + len(extra): 1} if ahead is not None else {},
            compiler_params=params,
            cost_estimate=cost(2**24, 2**22),
            name="fold",
        )(*operands, *after)
        return result if ahead is not None else (result[0], None)

    folded, cross_got, hiddens, full_got = {}, {}, {}, {}

    def stage_fold(c, *after):
        part = parts[c]
        for s, pairs in enumerate(fold):
            got = first_got[c] if s == 0 else tp_send(part, pairs)
            ahead = parts.get(c + 2) if s == 0 and c + 2 not in first_got else None
            part, ahead = fold_call(c if s == 0 else count, part, got, ahead, *after)
            if ahead is not None:
                parts[c + 2] = ahead
        folded[c] = part
        cross_got[c] = tp_send(part, across)

    ends, first = {}, 0
    for size in GROUPS:
        last = min(first + size, count) - 1
        if last >= first:
            ends[last] = first
        first = last + 1
    if count - 1 not in ends:
        ends[count - 1] = first

    def stage_hidden(c, *after):
        earlier = list(range(ends[c], c)) if c in ends else []
        width = sum(widths[n] for n in earlier + [c])
        hidden = small(
            functools.partial(hidden_kernel, tile, len(earlier)),
            "hidden",
            (entries, width),
            [folded[c], cross_got[c]] + [hiddens[n] for n in earlier],
            *after,
        )
        hiddens[c] = hidden
        if c not in ends:
            return
        for s, pairs in enumerate(unfold):
            got = tp_send(hidden, pairs)
            if s < len(unfold) - 1:
                fresh = (tp_index == inner - 2 - s) | (tp_index == inner + s + 1)
                hidden = jnp.where(fresh, got, hidden)
        full_got[c] = (hidden, got)

    outermost = (tp_index == 0) | (tp_index == tp - 1)

    def stage_down(c, total, *after):
        hidden, got = full_got[c]
        hidden = gated(jnp.where(outermost, got, hidden), *after)
        rows_of = slice(spans[ends[c]][0], spans[c][1])
        value = jnp.dot(hidden, down_weight[rows_of], preferred_element_type=f32)
        return value if total is None else total + value

    latest, total = [], None
    for t in range(count + 2):
        if t < count:
            stage_fold(t, *latest)
            latest = [folded[t]]
        if t + 2 < count:
            parts[t + 2] = project(t + 2, *latest)
            latest = [parts[t + 2]]
            first_got[t + 2] = tp_send(parts[t + 2], fold[0])
        for c in (t - 1, t):
            ahead = c + 1 < count and bool(AHEAD[c])
            if 0 <= c < count and ahead == (c == t):
                stage_hidden(c, *latest)
                latest = [hiddens[c]]
        if t - 2 in ends:
            total = stage_down(t - 2, total, *latest)
            latest = [total]

    total = total.reshape(steps, rows, out_feat)
    got = dp_xor(total[:, rows // 2 :].astype(bf16), 1)
    pair = total[:, : rows // 2] + got.astype(f32)
    pair_sent = pair.astype(bf16)
    mixed = pair[:, :home]
    for e in range(1, dp // 2):
        mixed = mixed + dp_xor(pair_sent[:, e * home : (e + 1) * home], 2 * e).astype(f32)
    mixed = mixed.astype(bf16)
    return mixed


def solution(mesh):
    placed = (
        P(None, "dp", "tensor"),
        P("tensor", "dp"),
        P("tensor", "dp"),
        P("dp", "tensor"),
        P("tensor", "dp"),
        P(None, "tensor", None, "dp"),
        P("dp"),
        P(),
    )
    return jax.shard_map(
        per_device, mesh=mesh, in_specs=placed, out_specs=P(None, "dp", "tensor"), check_vma=False
    )
```

```python
import functools
import jax
import jax.numpy as jnp
from jax import lax
from jax.experimental import pallas as pl
from jax.experimental.pallas import tpu as pltpu
from jax.sharding import PartitionSpec as P

SHARES = (1, 2, 3, 3, 3, 2)
GROUPS = (1, 1, 1, 1, 1, 1, 1)
AHEAD = (1, 1, 0, 0, 0)
EARLY = 2
LIMIT = 24 * 1024 * 1024
PROJECT_LIMIT = 50 * 1024 * 1024


def transposed_dot(lows, maps):
    return lax.dot_general(lows, maps, (((0,), (0,)), ((), ())), preferred_element_type=jnp.float32)


def exact_dot(left, right):
    return jnp.dot(
        left, right, precision=lax.Precision.HIGHEST, preferred_element_type=jnp.float32
    )


def local_order(home, rows, entries, dp, dp_index):
    entry = lax.broadcasted_iota(jnp.int32, (entries, entries), 0)
    target = lax.broadcasted_iota(jnp.int32, (entries, entries), 1)
    local_row = entry % rows
    slot = local_row // home
    relative = jnp.where(slot < dp // 2, 2 * slot, 2 * slot - dp + 1)
    true_row = jnp.bitwise_xor(relative, dp_index) * home + local_row % home
    return (entry - local_row + true_row == target).astype(jnp.float32)


def shrink_kernel(home, dp, where_ref, scale_ref, x_ref, shrink_ref, ids_ref, *rest):
    out_ref = rest[-1]
    entries = x_ref.shape[0]
    wide = out_ref.shape[0]
    owner = where_ref[0]
    shrunk = lax.dot_general(
        shrink_ref[...], x_ref[...], (((0,), (1,)), ((), ())), preferred_element_type=jnp.float32
    )
    total = jnp.zeros(out_ref.shape, jnp.float32)
    order = local_order(home, home * dp, entries, dp, owner)
    ordered = exact_dot(shrunk, order)
    held = scale_ref.shape[0]
    for a in range(held):
        mine = jnp.where(ids_ref[...] == owner * held + a, scale_ref[a], 0.0)
        total = total + ordered[wide * a : wide * (a + 1)] * mine
    out_ref[...] = total


def lows_kernel(home, dp, count, rank, adapters, where_ref, ids_ref, *refs):
    low = refs[0][...]
    for ref in refs[1:count]:
        low = low + ref[...]
    out_ref = refs[-1]
    entries = low.shape[1]
    low = low.astype(jnp.bfloat16).astype(jnp.float32)
    order = local_order(home, home * dp, entries, dp, where_ref[0]).astype(jnp.bfloat16)
    depth = adapters * rank
    holder = lax.broadcasted_iota(jnp.int32, (depth, entries), 0) // rank
    for place in range(2):
        member = ids_ref[...] == where_ref[1 + place] * adapters + holder
        for j in range(2):
            tiled = jnp.concatenate([low[rank * j : rank * (j + 1)]] * adapters, axis=0)
            chosen = jnp.where(member, tiled, 0.0).astype(jnp.bfloat16)
            out_ref[j, depth * place : depth * (place + 1)] = lax.dot_general(
                chosen, order, (((1,), (1,)), ((), ())), preferred_element_type=jnp.float32
            ).astype(jnp.bfloat16)


def project_kernel(with_lows, x_ref, gate_ref, up_ref, *rest):
    out_ref = rest[-1]
    for j, weight_ref in enumerate((gate_ref, up_ref)):
        value = jnp.dot(x_ref[...], weight_ref[...], preferred_element_type=jnp.float32)
        if with_lows:
            depth = rest[1].shape[1]
            value = value + transposed_dot(rest[0][j, :depth], rest[1][j])
        out_ref[j] = value.astype(out_ref.dtype)


def fold_kernel(tile, first, maps, outputs, part_ref, got_ref, *rest):
    out_ref = rest[len(rest) - outputs]
    for lo in range(0, out_ref.shape[2], tile):
        cols = slice(lo, lo + tile)
        for j in range(2):
            value = part_ref[j, :, cols].astype(jnp.float32) + got_ref[j, :, cols].astype(jnp.float32)
            for n in range(maps):
                depth = rest[1 + n].shape[1]
                value = value + transposed_dot(
                    rest[0][j, depth * n : depth * (n + 1)],
                    rest[1 + n][j, :, first + lo : first + lo + tile],
                )
            out_ref[j, :, cols] = value.astype(out_ref.dtype)


def hidden_kernel(tile, earlier, part_ref, *rest):
    out_ref = rest[-1]
    first = 0
    for ref in rest[1 : 1 + earlier]:
        width = ref.shape[1]
        out_ref[:, first : first + width] = ref[...]
        first += width
    for lo in range(0, part_ref.shape[2], tile):
        cols = slice(lo, lo + tile)
        gate, up = part_ref[0, :, cols].astype(jnp.float32), part_ref[1, :, cols].astype(jnp.float32)
        if rest[0].shape == part_ref.shape:
            gate = gate + rest[0][0, :, cols].astype(jnp.float32)
            up = up + rest[0][1, :, cols].astype(jnp.float32)
        place = slice(first + lo, first + lo + tile)
        out_ref[:, place] = (gate / (1.0 + jnp.exp(-gate)) * up).astype(out_ref.dtype)


def per_device(
    activations,
    gate_weight,
    up_weight,
    down_weight,
    shrink_weight,
    expand_weight,
    adapter_scale,
    adapter_ids,
):
    f32, bf16 = jnp.float32, jnp.bfloat16
    dp, tp = lax.axis_size("dp"), lax.axis_size("tensor")
    dp_index, tp_index = lax.axis_index("dp"), lax.axis_index("tensor")
    steps, home, feat = activations.shape
    rows = home * dp
    entries = steps * rows
    adp_block, low_rank, ff_local = expand_weight.shape[1:]
    depth = adp_block * low_rank
    out_feat = down_weight.shape[1]
    number = lambda value: jnp.asarray(value, jnp.int32).reshape(1)
    inner = tp // 2
    tile = 256 if ff_local % 256 == 0 else 128

    def dp_xor(value, k):
        return lax.ppermute(value, "dp", [(s, s ^ k) for s in range(dp)])

    def tp_send(value, pairs):
        return lax.ppermute(value, "tensor", pairs)

    def gated(value, *others):
        return lax.optimization_barrier((value,) + others)[0] if others else value

    groups, done, bounds = ff_local // tile, 0, [0]
    for share in SHARES:
        done += share
        bounds.append(groups * done // sum(SHARES) * tile)
    spans = [(lo, hi) for lo, hi in zip(bounds[:-1], bounds[1:]) if hi > lo]
    widths = [hi - lo for lo, hi in spans]
    count = len(spans)
    fold = [[(s, s + 1), (tp - 1 - s, tp - 2 - s)] for s in range(inner - 1)]
    across = [(inner - 1, inner), (inner, inner - 1)]
    unfold = [[(inner - 1 - s, inner - 2 - s), (inner + s, inner + s + 1)] for s in range(inner - 1)]

    params = pltpu.CompilerParams(vmem_limit_bytes=LIMIT)
    scalar = pl.BlockSpec(memory_space=pltpu.SMEM)
    anywhere = pl.BlockSpec(memory_space=pl.ANY)

    def whole(value):
        return pl.BlockSpec(value.shape, lambda *t: (0,) * value.ndim)

    def cost(flops, nbytes):
        return pl.CostEstimate(flops=1, bytes_accessed=1, transcendentals=0)

    even = [activations] + [dp_xor(activations, k) for k in range(2, dp, 2)]
    odd = [dp_xor(value, 1) for value in even]
    x_all = jnp.concatenate(even + odd, axis=1).reshape(entries, feat)

    expand = expand_weight.reshape(2, depth, ff_local)
    early = min(EARLY, count - 1)
    maps = [expand[:, :, : spans[early - 1][1]]]
    maps.append(tp_send(maps[0], fold[0]))
    away = jnp.where(tp_index < inner, tp_index - 1, tp_index + 1)

    def project(c, *after):
        lo, hi = spans[c]
        wide = 2 * tile if lo % (2 * tile) == 0 and hi % (2 * tile) == 0 else tile
        first = lo // wide
        weights = pl.BlockSpec((feat, wide), lambda t: (0, first + t))
        operands, specs = [x_all, gate_weight, up_weight], [whole(x_all), weights, weights]
        if c >= early:
            operands += [lows, expand]
            specs += [whole(lows), pl.BlockSpec((2, depth, wide), lambda t: (0, 0, first + t))]
        return pl.pallas_call(
            functools.partial(project_kernel, c >= early),
            grid=((hi - lo) // wide,),
            in_specs=specs + [anywhere] * len(after),
            out_specs=pl.BlockSpec((2, entries, wide), lambda t: (0, 0, t)),
            out_shape=jax.ShapeDtypeStruct((2, entries, hi - lo), bf16),
            compiler_params=pltpu.CompilerParams(vmem_limit_bytes=PROJECT_LIMIT),
            cost_estimate=cost(4 * entries * feat * (hi - lo), 8 * feat * (hi - lo)),
            name="project",
        )(*operands, *after)

    global_ids = jnp.tile(adapter_ids, (steps,)).reshape(1, entries)
    partial = pl.pallas_call(
        functools.partial(shrink_kernel, home, dp),
        in_specs=[scalar, scalar, whole(x_all), whole(shrink_weight), whole(global_ids), anywhere],
        out_specs=pl.BlockSpec((2 * low_rank, entries), lambda: (0, 0)),
        out_shape=jax.ShapeDtypeStruct((2 * low_rank, entries), f32),
        compiler_params=params,
        cost_estimate=cost(2**27, 2**21),
        name="shrink",
    )(number(dp_index), adapter_scale, x_all, shrink_weight, global_ids, global_ids)
    parts = {0: project(0, partial)}
    first_got = {0: tp_send(parts[0], fold[0])}
    low = functools.reduce(
        jnp.add, [gated(partial, parts[0])] + [tp_send(partial, [(s, s ^ k) for s in range(tp)]) for k in range(1, tp)]
    )
    for c in range(1, early):
        parts[c] = project(c, low, maps[1])
        first_got[c] = tp_send(parts[c], fold[0])
    low = functools.reduce(
        jnp.add, [gated(low, parts[early - 1])] + [dp_xor(low, k) for k in range(2, dp, 2)]
    )
    pieces = [low, dp_xor(low, 1)]
    lows = pl.pallas_call(
        functools.partial(lows_kernel, home, dp, len(pieces), low_rank, adp_block),
        in_specs=[scalar, whole(global_ids)] + [whole(low)] * len(pieces),
        out_specs=pl.BlockSpec((2, 2 * depth, entries), lambda: (0, 0, 0)),
        out_shape=jax.ShapeDtypeStruct((2, 2 * depth, entries), bf16),
        compiler_params=params,
        cost_estimate=cost(2**27, 2**20),
        name="lows",
    )(
        jnp.concatenate([number(dp_index), number(tp_index), number(away)]), global_ids, *pieces
    )

    def small(kernel, name, shape, operands, *after):
        return pl.pallas_call(
            kernel,
            in_specs=[whole(value) for value in operands] + [anywhere] * len(after),
            out_specs=pl.BlockSpec(shape, lambda: (0,) * len(shape)),
            out_shape=jax.ShapeDtypeStruct(shape, bf16),
            compiler_params=params,
            cost_estimate=cost(2**24, 2**22),
            name=name,
        )(*operands, *after)

    def fold_call(c, part, got, ahead, *after):
        shapes = [jax.ShapeDtypeStruct(part.shape, bf16)]
        operands = [part, got]
        specs = [whole(part), whole(got)]
        outs = [pl.BlockSpec(part.shape, lambda: (0,) * part.ndim)]
        extra = [lows] + maps if c < early else []
        operands += extra
        specs += [whole(value) for value in extra]
        if ahead is not None:
            operands.append(ahead)
            specs.append(anywhere)
            outs.append(anywhere)
            shapes.append(jax.ShapeDtypeStruct(ahead.shape, bf16))
        result = pl.pallas_call(
            functools.partial(
                fold_kernel, tile, spans[c][0] if extra else 0, len(extra[1:]), len(outs)
            ),
            in_specs=specs + [anywhere] * len(after),
            out_specs=outs,
            out_shape=shapes,
            input_output_aliases={2 + len(extra): 1} if ahead is not None else {},
            compiler_params=params,
            cost_estimate=cost(2**24, 2**22),
            name="fold",
        )(*operands, *after)
        return result if ahead is not None else (result[0], None)

    folded, cross_got, hiddens, full_got = {}, {}, {}, {}

    def stage_fold(c, *after):
        part = parts[c]
        for s, pairs in enumerate(fold):
            got = first_got[c] if s == 0 else tp_send(part, pairs)
            ahead = parts.get(c + 2) if s == 0 and c + 2 not in first_got else None
            part, ahead = fold_call(c if s == 0 else count, part, got, ahead, *after)
            if ahead is not None:
                parts[c + 2] = ahead
        folded[c] = part
        cross_got[c] = tp_send(part, across)

    ends, first = {}, 0
    for size in GROUPS:
        last = min(first + size, count) - 1
        if last >= first:
            ends[last] = first
        first = last + 1
    if count - 1 not in ends:
        ends[count - 1] = first

    def stage_hidden(c, *after):
        earlier = list(range(ends[c], c)) if c in ends else []
        width = sum(widths[n] for n in earlier + [c])
        hidden = small(
            functools.partial(hidden_kernel, tile, len(earlier)),
            "hidden",
            (entries, width),
            [folded[c], cross_got[c]] + [hiddens[n] for n in earlier],
            *after,
        )
        hiddens[c] = hidden
        if c not in ends:
            return
        for s, pairs in enumerate(unfold):
            got = tp_send(hidden, pairs)
            if s < len(unfold) - 1:
                fresh = (tp_index == inner - 2 - s) | (tp_index == inner + s + 1)
                hidden = jnp.where(fresh, got, hidden)
        full_got[c] = (hidden, got)

    outermost = (tp_index == 0) | (tp_index == tp - 1)

    def stage_down(c, total, *after):
        hidden, got = full_got[c]
        hidden = gated(jnp.where(outermost, got, hidden), *after)
        rows_of = slice(spans[ends[c]][0], spans[c][1])
        value = jnp.dot(hidden, down_weight[rows_of], preferred_element_type=f32)
        return value if total is None else total + value

    latest, total = [], None
    for t in range(count + 2):
        if t < count:
            stage_fold(t, *latest)
            latest = [folded[t]]
        if t + 2 < count:
            parts[t + 2] = project(t + 2, *latest)
            latest = [parts[t + 2]]
            first_got[t + 2] = tp_send(parts[t + 2], fold[0])
        for c in (t - 1, t):
            ahead = c + 1 < count and bool(AHEAD[c])
            if 0 <= c < count and ahead == (c == t):
                stage_hidden(c, *latest)
                latest = [hiddens[c]]
        if t - 2 in ends:
            total = stage_down(t - 2, total, *latest)
            latest = [total]

    total = total.reshape(steps, rows, out_feat)
    got = dp_xor(total[:, rows // 2 :].astype(bf16), 1)
    pair = total[:, : rows // 2] + got.astype(f32)
    pair_sent = pair.astype(bf16)
    mixed = pair[:, :home]
    for e in range(dp // 2 - 1, 0, -1):
        mixed = mixed + dp_xor(pair_sent[:, e * home : (e + 1) * home], 2 * e).astype(f32)
    mixed = mixed.astype(bf16)
    return mixed


def solution(mesh):
    placed = (
        P(None, "dp", "tensor"),
        P("tensor", "dp"),
        P("tensor", "dp"),
        P("dp", "tensor"),
        P("tensor", "dp"),
        P(None, "tensor", None, "dp"),
        P("dp"),
        P(),
    )
    return jax.shard_map(
        per_device, mesh=mesh, in_specs=placed, out_specs=P(None, "dp", "tensor"), check_vma=False
    )
```
